512 devices in a mesh: prow: 16 (over z_hi, x), pcol: 32 (over y, z_lo, core).
Axes of the slice: x: 4, y: 8, z: 8 (z_hi: 4, z_lo: 2; z = z_hi * 2 + z_lo), core: 2. Of those that a mesh axis runs over, the one named last changes fastest.
Arguments:
- matrix: bfloat16 [16384, 16384], P('prow', 'pcol'), may hold values from -6 to 6
- panels: bfloat16 [6, 16384, 256], P(None, ('prow', 'pcol')), may hold values from -0.375 to 0.375
- diag_blocks: float32 [6, 256, 256], replicated, may hold values from -0.1875 to 0.1875
- pivots: int32 [6, 256], replicated, may hold values from 0 to 16383, as said below
Outputs:
- updated: bfloat16 [16384, 16384], P('prow', 'pcol')
The draws below stay inside these ranges and needn't reach their ends.
Inputs may be any that keep to these rules, and one draw needn't show every extreme that they name: `pivots`: within one step the 256 pivot rows are distinct, and no pivot row lies in a diagonal block row of any of the 6 steps.
All inputs are finite; a program needn't handle non-finite values.
Results may differ from the reference program's by a relative error of at most 0.0091.
Values may be sent and summed in bfloat16 or wider, within the bound.
No kernel may reach another device: no remote copies, remote signals or barrier semaphores. Data moves between devices by JAX's collectives and lax.ppermute only.
A program may use at most 64 MiB of HBM per device.

```python
import jax
import jax.numpy as jnp
from jax import lax

NB = 256
RDEV = 1024
STEPS = 6
ROWS = 16384
COLS = 16384
N_PROW = 16


def draw_pivots(key, part):
    key = jax.random.fold_in(key, 7)
    row_ids = jnp.arange(ROWS, dtype=jnp.int32)
    taken = jnp.zeros((ROWS,), jnp.int32)
    for step in range(STEPS):
        start = step % N_PROW * RDEV + step // N_PROW * NB
        taken = taken + ((row_ids >= start) & (row_ids < start + NB)).astype(jnp.int32)
    free_count = ROWS - STEPS * NB
    allowed = jnp.nonzero(taken == 0, size=free_count)[0].astype(jnp.int32)
    lists = []
    for step in range(STEPS):
        order = jax.random.permutation(jax.random.fold_in(key, step), free_count)[:NB]
        lists.append(allowed[order])
    return jnp.stack(lists).astype(jnp.int32)


def block_scale(rng, shape, split, low, top_value):
    def one(dim, parts):
        steps = jax.random.uniform(jax.random.fold_in(jax.random.fold_in(rng, 6), dim), (parts,), jnp.float32, low / len(split), top_value / len(split))
        return jnp.repeat(jnp.exp(steps), shape[dim] // parts).reshape((-1,) + (1,) * (len(shape) - dim - 1))

    level = one(*split[0])
    for cut in split[1:]:
        level = level * one(*cut)
    return level


def bell_draw(own_key, shape, width, reach, pieces=(), kind=jnp.bfloat16):
    loudness = block_scale(own_key, shape, pieces, -0.22, 0.18) if pieces else 1.0
    drawn = jax.random.normal(own_key, shape, jnp.float32) * width * loudness
    return jnp.minimum(jnp.maximum(drawn, -reach), reach).astype(kind)


def setup_inputs(seed: int = 0) -> dict:
    key_of = jax.random.split(jax.random.key(seed), 5)
    matrix = bell_draw(key_of[0], (ROWS, COLS), 1.0, 6.0, ((0, 16), (1, 32)))
    panels = bell_draw(key_of[1], (STEPS, ROWS, NB), NB ** -0.5, 0.375, ((1, 512),))
    diag_blocks = bell_draw(key_of[2], (STEPS, NB, NB), (4 * NB) ** -0.5, 0.1875, (), jnp.float32)
    pivots = draw_pivots(jax.random.fold_in(key_of[4], 71), 0)
    return dict(matrix=matrix, panels=panels, diag_blocks=diag_blocks, pivots=pivots)


def top_start(step):
    return step % N_PROW * RDEV + step // N_PROW * NB

def reference(matrix, panels, diag_blocks, pivots):
    current = matrix
    row_ids = jnp.arange(ROWS, dtype=jnp.int32)
    finished = jnp.zeros((ROWS,), dtype=bool)
    for step in range(STEPS):
        start = top_start(step)
        old_rows = current[start:start + NB]
        new_top = current[pivots[step]]
        current = current.at[pivots[step]].set(old_rows)
        solved = lax.linalg.triangular_solve(diag_blocks[step], new_top.astype(jnp.float32), left_side=True, lower=True, unit_diagonal=True)
        upper = solved.astype(jnp.bfloat16)
        finished = finished | (row_ids >= start) & (row_ids < start + NB)
        product = jnp.dot(panels[step].astype(jnp.float32), upper.astype(jnp.float32), preferred_element_type=jnp.float32)
        changed = (current.astype(jnp.float32) - product).astype(jnp.bfloat16)
        current = jnp.where(finished[:, None], current, changed)
        current = current.at[start:start + NB].set(upper)
    return current
```

```python
import jax
import jax.numpy as jnp
from jax import lax
from jax.experimental import pallas as pl
from jax.experimental.pallas import tpu as pltpu
from jax.sharding import Mesh
from jax.sharding import PartitionSpec as P

STEPS = 6
NB = 256
ROWS = 1024
FINE = ("zh", "x", "y", "zl", "c")
PAIRS = [(s, k) for k in range(STEPS) for s in range(k + 1, STEPS)]


def split(v):
    high = v.astype(jnp.bfloat16)
    return high, (v - high.astype(jnp.float32)).astype(jnp.bfloat16)


def dot(a, b):
    return jnp.dot(a, b, preferred_element_type=jnp.float32)


def dot3(a, b):
    ah, al = split(a)
    bh, bl = split(b)
    return dot(ah, bh) + (dot(ah, bl) + dot(al, bh))


def inverse_kernel(l_ref, high_ref, low_ref):
    row = lax.broadcasted_iota(jnp.int32, (NB, NB), 0)
    col = lax.broadcasted_iota(jnp.int32, (NB, NB), 1)
    eye = (row == col).astype(jnp.float32)
    lower = [l_ref[s] for s in range(STEPS)]
    inv = [eye] * STEPS
    size = 1
    while size < NB:
        joins = (row // (2 * size) == col // (2 * size)) & (row // size > col // size)
        parts = [jnp.where(joins, m, 0.0) for m in lower]
        if size == 1:
            inv = [eye - m for m in parts]
        else:
            left = [dot3(m, x) for m, x in zip(parts, inv)]
            inv = [x - dot3(x, m) for x, m in zip(inv, left)]
        size *= 2
    for s in range(STEPS):
        high_ref[s], low_ref[s] = split(inv[s])


def inverses(diag_blocks):
    out = jax.ShapeDtypeStruct((STEPS, NB, NB), jnp.bfloat16)
    spec = pl.BlockSpec(memory_space=pltpu.VMEM)
    return pl.pallas_call(
        inverse_kernel,
        out_shape=(out, out),
        in_specs=[spec],
        out_specs=(spec, spec),
        compiler_params=pltpu.CompilerParams(vmem_limit_bytes=48 * 2**20),
        cost_estimate=pl.CostEstimate(flops=2 * 42 * 6 * NB**3, bytes_accessed=3 * 2**20, transcendentals=0),
    )(diag_blocks)


def exchange(v, axis):
    return lax.all_to_all(v, axis, 0, 0)


def everyone(v, axis):
    n = lax.axis_size(axis)
    return exchange(jnp.broadcast_to(v[None], (n,) + v.shape), axis)


def add_up(v):
    return jnp.sum(v.astype(jnp.float32), axis=0).astype(v.dtype)


def swap(v, axis):
    other = lax.ppermute(v, axis, [(0, 1), (1, 0)])
    first = lax.axis_index(axis) == 0
    return jnp.stack([jnp.where(first, v, other), jnp.where(first, other, v)])


def picks(ids, held):
    return (ids[:, None] == held[None, :]).astype(jnp.bfloat16)


def body(matrix, panels, diag_blocks, pivots):
    width = matrix.shape[1]
    zh, x, y = lax.axis_index("zh"), lax.axis_index("x"), lax.axis_index("y")
    zl, c = lax.axis_index("zl"), lax.axis_index("c")
    me = zh * 4 + x
    first = me * ROWS

    same = pivots[:, :, None, None] == pivots[None, None]
    t_ids = jnp.arange(STEPS, dtype=jnp.int32)
    i_ids = jnp.arange(NB, dtype=jnp.int32)
    before = (t_ids[None, :] < t_ids[:, None])[:, None, :, None]
    code = jnp.where(same & before, t_ids[:, None] * ROWS + i_ids[None, :], -1)
    origin = jnp.max(code, axis=(2, 3))
    base = jnp.where(origin >= 0, origin, pivots)
    swapped_at = jnp.where(origin >= 0, origin // ROWS, -1)

    high, low = inverses(diag_blocks)

    by_y = everyone(panels, "y")
    mine = by_y.transpose(1, 0, 2, 3).reshape(STEPS, 8 * 32, NB)
    held = (
        first
        + (jnp.arange(8, dtype=jnp.int32) * 128)[:, None]
        + zl * 64
        + c * 32
        + jnp.arange(32, dtype=jnp.int32)[None, :]
    ).reshape(-1)

    j_y = y * 32 + jnp.arange(32, dtype=jnp.int32)
    piv_y = lax.dynamic_slice_in_dim(pivots, y * 32, 32, 1)
    org_y = lax.dynamic_slice_in_dim(origin, y * 32, 32, 1)
    at_y = lax.dynamic_slice_in_dim(swapped_at, y * 32, 32, 1)
    parts = []
    for k in range(STEPS - 1):
        later = slice(k + 1, STEPS)
        l_ids = jnp.where(at_y[later] > k, org_y[later], piv_y[later])
        d_ids = (t_ids[later] * ROWS)[:, None] + j_y[None, :]
        ids = jnp.stack([l_ids, d_ids], axis=1).reshape(-1)
        parts.append(dot(picks(ids, held), mine[k]).astype(jnp.bfloat16))
    rows = jnp.concatenate(parts).reshape(15, 2, 4, 8, NB).transpose(2, 0, 1, 3, 4)
    chunk = add_up(exchange(rows, ("zl", "c")))
    chunk = add_up(everyone(chunk, "x"))
    chunk = add_up(everyone(chunk, "zh"))
    chunk = swap(swap(everyone(chunk, "y"), "zl"), "c")
    blocks = chunk.transpose(3, 4, 2, 1, 0, 5, 6).reshape(15, 2, NB, NB)

    whole = swap(swap(by_y, "zl"), "c")
    whole = whole.transpose(3, 2, 1, 0, 4, 5).reshape(STEPS, ROWS, NB)

    local = first + jnp.arange(ROWS, dtype=jnp.int32)
    picked = dot(picks(base.reshape(-1), local), matrix).astype(jnp.bfloat16)
    picked = picked.reshape(STEPS, 4, 64, width).transpose(1, 0, 2, 3)
    diag = matrix[:NB].reshape(4, 1, 64, width)
    part = exchange(jnp.concatenate([picked, diag], axis=1), "x")
    some = add_up(part[:, :STEPS])
    both = jnp.concatenate([some, part[:, STEPS]], axis=0).reshape(10, 4, 16, width).transpose(1, 0, 2, 3)
    part = exchange(both, "zh")
    active = jnp.concatenate([add_up(part[:, :STEPS]), part[0, STEPS:], part[1, STEPS : STEPS + 2]])
    active = everyone(everyone(active, "zh"), "x")
    active = active.transpose(2, 0, 1, 3, 4).reshape(2, STEPS, NB, width)

    tops = [active[0, s] for s in range(STEPS)]
    olds = [active[1, s] for s in range(STEPS)]
    current = matrix
    uppers = []
    place = {pair: n for n, pair in enumerate(PAIRS)}

    def less(a, b, u):
        return (a.astype(jnp.float32) - dot(b, u)).astype(jnp.bfloat16)

    for s in range(STEPS):
        u = (dot(high[s], tops[s]) + dot(low[s], tops[s])).astype(jnp.bfloat16)
        uppers.append(u)
        for t in range(s + 1, STEPS):
            n = place[(t, s)]
            tops[t] = less(tops[t], blocks[n, 0], u)
            olds[t] = less(olds[t], blocks[n, 1], u)
        put = picks(local, pivots[s])
        hit = jnp.any(put > 0, axis=1)
        moved = dot(put, olds[s]).astype(jnp.bfloat16)
        current = less(jnp.where(hit[:, None], moved, current), whole[s], u)
    own = lax.dynamic_index_in_dim(jnp.stack(uppers), jnp.minimum(me, STEPS - 1), 0, keepdims=False)
    head = jnp.where(me < STEPS, own, current[:NB])
    return jnp.concatenate([head, current[NB:]])


def solution(mesh):
    fine = Mesh(mesh.devices.reshape(4, 4, 8, 2, 2), FINE)
    prow, pcol = ("zh", "x"), ("y", "zl", "c")
    return jax.shard_map(
        body,
        mesh=fine,
        in_specs=(P(prow, pcol), P(None, prow + pcol, None), P(), P()),
        out_specs=P(prow, pcol),
        check_vma=False,
    )
```

```python
import jax
import jax.numpy as jnp
from jax import lax
from jax.experimental import pallas as pl
from jax.experimental.pallas import tpu as pltpu
from jax.sharding import Mesh
from jax.sharding import PartitionSpec as P

STEPS = 6
NB = 256
ROWS = 1024
FINE = ("zh", "x", "y", "zl", "c")
PAIRS = [(s, k) for k in range(STEPS) for s in range(k + 1, STEPS)] + [(0, 0)]
PLACE = {pair: n for n, pair in enumerate(PAIRS)}
SLOTS = 32


def split(v):
    high = v.astype(jnp.bfloat16)
    return high, (v - high.astype(jnp.float32)).astype(jnp.bfloat16)


def dot(a, b):
    return jnp.dot(a, b, preferred_element_type=jnp.float32)


def dot3(a, b):
    ah, al = split(a)
    bh, bl = split(b)
    return dot(ah, bh) + (dot(ah, bl) + dot(al, bh))


def inverse_kernel(l_ref, high_ref, low_ref):
    row = lax.broadcasted_iota(jnp.int32, (NB, NB), 0)
    col = lax.broadcasted_iota(jnp.int32, (NB, NB), 1)
    eye = (row == col).astype(jnp.float32)
    lower = [l_ref[s] for s in range(STEPS)]
    inv = [eye] * STEPS
    size = 1
    while size < NB:
        joins = (row // (2 * size) == col // (2 * size)) & (row // size > col // size)
        parts = [jnp.where(joins, m, 0.0) for m in lower]
        if size == 1:
            inv = [eye - m for m in parts]
        else:
            left = [dot3(m, x) for m, x in zip(parts, inv)]
            inv = [x - dot3(x, m) for x, m in zip(inv, left)]
        size *= 2
    for s in range(STEPS):
        high_ref[s], low_ref[s] = split(inv[s])


def inverses(diag_blocks):
    out = jax.ShapeDtypeStruct((STEPS, NB, NB), jnp.bfloat16)
    spec = pl.BlockSpec(memory_space=pltpu.VMEM)
    return pl.pallas_call(
        inverse_kernel,
        out_shape=(out, out),
        in_specs=[spec],
        out_specs=(spec, spec),
        compiler_params=pltpu.CompilerParams(vmem_limit_bytes=48 * 2**20),
        cost_estimate=pl.CostEstimate(flops=2 * 42 * 6 * NB**3, bytes_accessed=3 * 2**20, transcendentals=0),
    )(diag_blocks)


def exchange(v, axis):
    return lax.all_to_all(v, axis, 0, 0)


def everyone(v, axis):
    n = lax.axis_size(axis)
    return exchange(jnp.broadcast_to(v[None], (n,) + v.shape), axis)


def add_up(v):
    return jnp.sum(v.astype(jnp.float32), axis=0).astype(v.dtype)


def shift(v, axis, by):
    n = lax.axis_size(axis)
    return lax.ppermute(v, axis, [(i, (i + by) % n) for i in range(n)])


def dealt(v, axis):
    n, at = lax.axis_size(axis), lax.axis_index(axis)
    parts = [lax.dynamic_index_in_dim(v, (at + d) % n, 0, keepdims=False) for d in range(n)]
    return parts[:1] + [shift(parts[d], axis, d) for d in range(1, n)]


def passed(v, axis):
    return [v] + [shift(v, axis, d) for d in range(1, lax.axis_size(axis))]


def picks(ids, held):
    return (ids[:, None] == held[None, :]).astype(jnp.bfloat16)


def l_rows_kernel(at_ref, ts_ref, ks_ref, ids_ref, panels_ref, out_ref):
    zh, x, zl, c = at_ref[0], at_ref[1], at_ref[2], at_ref[3]
    lane = lax.broadcasted_iota(jnp.int32, (NB, 64), 0)
    held = (zh * 4 + x) * ROWS + zl * 64 + c * 32 + lane // 32 * 128 + lane % 32
    for m in range(8):
        t, k = ts_ref[m], ks_ref[m]
        put = jnp.where(held == ids_ref[pl.ds(k * STEPS + t, 1), :], 1.0, 0.0).astype(jnp.bfloat16)
        mine = panels_ref[:, pl.ds(k, 1)].reshape(NB, NB)
        rows = lax.dot_general(put, mine, (((0,), (0,)), ((), ())), preferred_element_type=jnp.float32)
        out_ref[:, m // 2, :, m % 2 * NB : m % 2 * NB + NB] = rows.astype(jnp.bfloat16).reshape(4, 16, NB)


def l_rows(at, ts, ks, ids, panels):
    vmem, smem = pl.BlockSpec(memory_space=pltpu.VMEM), pl.BlockSpec(memory_space=pltpu.SMEM)
    return pl.pallas_call(
        l_rows_kernel,
        out_shape=jax.ShapeDtypeStruct((4, 4, 16, 2 * NB), jnp.bfloat16),
        in_specs=[smem, smem, smem, vmem, vmem],
        out_specs=vmem,
        compiler_params=pltpu.CompilerParams(vmem_limit_bytes=16 * 2**20),
        cost_estimate=pl.CostEstimate(flops=2 * 8 * 64 * NB * NB, bytes_accessed=2**20, transcendentals=0),
    )(at, ts, ks, ids, panels)


def turned(zl, c, n):
    return lax.rem(zl + n // 2, 2), lax.rem(c + n % 2, 2)


def solve_kernel(at_ref, slot_ref, high_ref, low_ref, diag_ref, *refs):
    active_in, blocks_in, panels_in = refs[:4], refs[4:8], refs[8:12]
    u_ref, old_ref, send_ref, active, blocks, panels, active_sem, blocks_sem, panels_sem = refs[12:]
    zh, x, zl, c = at_ref[0], at_ref[1], at_ref[2], at_ref[3]
    me = zh * 4 + x
    width = diag_ref.shape[1]
    copies = []
    for d in range(4):
        for e in range(4):
            target = active.at[lax.rem(x - d + 4, 4), lax.rem(zh - e + 4, 4)]
            copies.append(pltpu.make_async_copy(active_in[d].at[e], target, active_sem.at[d * 4 + e]))
    for n in range(4):
        a, b = turned(zl, c, n)
        copies.append(pltpu.make_async_copy(blocks_in[n], blocks.at[:, a, b], blocks_sem.at[n]))
        copies.append(pltpu.make_async_copy(panels_in[n].at[0:2], panels.at[:, a, b], panels_sem.at[n]))
    for copy in copies:
        copy.start()
    for copy in copies:
        copy.wait()

    def rows_of(n):
        return active[:, :, n].reshape(NB, width)

    old_ref[...] = diag_ref[...]
    for s in range(STEPS):
        top = rows_of(s)
        u = (dot(high_ref[s], top) + dot(low_ref[s], top)).astype(jnp.bfloat16)
        u_ref[s] = u
        for t in range(s + 1, STEPS):
            n = PLACE[(t, s)]
            left = n // 2 % 2 * NB
            block = blocks[n % 2 * 4 : n % 2 * 4 + 4, :, :, n // 4, :, left : left + NB].reshape(NB, NB)
            less = rows_of(t).astype(jnp.float32) - dot(block, u)
            active[:, :, t] = less.astype(jnp.bfloat16).reshape(4, 4, 16, width)

        @pl.when(s < me)
        def _():
            panel = panels[:, :, :, s].reshape(NB, NB)
            old_ref[...] = (old_ref[...].astype(jnp.float32) - dot(panel, u)).astype(jnp.bfloat16)

    slot = lax.broadcasted_iota(jnp.int32, (16 * SLOTS, NB), 0)
    put = jnp.where(slot == slot_ref[...], 1.0, 0.0).astype(jnp.bfloat16)
    send_ref[...] = dot(put, old_ref[...]).astype(jnp.bfloat16)


def solve(at, slot, high, low, diag, active, blocks, panels):
    width = diag.shape[1]
    vmem, anywhere = pl.BlockSpec(memory_space=pltpu.VMEM), pl.BlockSpec(memory_space=pl.ANY)
    return pl.pallas_call(
        solve_kernel,
        out_shape=(
            jax.ShapeDtypeStruct((STEPS, NB, width), jnp.bfloat16),
            jax.ShapeDtypeStruct((NB, width), jnp.bfloat16),
            jax.ShapeDtypeStruct((16 * SLOTS, width), jnp.bfloat16),
        ),
        in_specs=[pl.BlockSpec(memory_space=pltpu.SMEM)] + [vmem] * 4 + [anywhere] * 12,
        out_specs=(vmem,) * 3,
        scratch_shapes=[
            pltpu.VMEM((4, 4, STEPS, 16, width), jnp.bfloat16),
            pltpu.VMEM((8, 2, 2, 4, 16, 2 * NB), jnp.bfloat16),
            pltpu.VMEM((2, 2, 2, STEPS, 32, NB), jnp.bfloat16),
            pltpu.SemaphoreType.DMA((16,)),
            pltpu.SemaphoreType.DMA((4,)),
            pltpu.SemaphoreType.DMA((4,)),
        ],
        compiler_params=pltpu.CompilerParams(vmem_limit_bytes=58 * 2**20),
        cost_estimate=pl.CostEstimate(flops=2 * 35 * NB * NB * width, bytes_accessed=9 * 2**20, transcendentals=0),
    )(at, slot, high, low, diag, *active, *blocks, *panels)


def update_kernel(at_ref, last_ref, u_ref, matrix_ref, *refs):
    panels_in, (out_ref, panels, panels_sem) = refs[:4], refs[4:]
    zl, c = at_ref[2], at_ref[3]
    width = matrix_ref.shape[1]
    copies = []
    for n in range(4):
        a, b = turned(zl, c, n)
        copies.append(pltpu.make_async_copy(panels_in[n], panels.at[:, a, b], panels_sem.at[n]))
    for copy in copies:
        copy.start()
    for copy in copies:
        copy.wait()
    tall = 256

    @pl.loop(0, ROWS // tall)
    def _(i):
        span = pl.ds(pl.multiple_of(i * tall, tall), tall)
        last = jnp.concatenate([last_ref[span, :]] * (width // 128), axis=1)
        rows = matrix_ref[span, :].astype(jnp.float32)
        for s in range(STEPS):
            panel = panels[pl.ds(i * (tall // 128), tall // 128), :, :, s].reshape(tall, NB)
            rows = jnp.where(last == s, 0.0, rows) - dot(panel, u_ref[s])
            rows = jnp.where(last >= 0, rows, rows.astype(jnp.bfloat16).astype(jnp.float32))
        out_ref[span, :] = rows


def update(at, last, u, matrix, panels):
    vmem, anywhere = pl.BlockSpec(memory_space=pltpu.VMEM), pl.BlockSpec(memory_space=pl.ANY)
    return pl.pallas_call(
        update_kernel,
        out_shape=jax.ShapeDtypeStruct(matrix.shape, jnp.float32),
        in_specs=[pl.BlockSpec(memory_space=pltpu.SMEM)] + [vmem] * 3 + [anywhere] * 4,
        out_specs=vmem,
        scratch_shapes=[pltpu.VMEM((8, 2, 2, STEPS, 32, NB), jnp.bfloat16), pltpu.SemaphoreType.DMA((4,))],
        compiler_params=pltpu.CompilerParams(vmem_limit_bytes=58 * 2**20),
        cost_estimate=pl.CostEstimate(
            flops=2 * matrix.size * STEPS * NB, bytes_accessed=8 * 2**20, transcendentals=0
        ),
    )(at, last, u, matrix, *panels)


def place_kernel(at_ref, own_ref, put_ref, got_ref, total_ref, out_ref):
    me = at_ref[0] * 4 + at_ref[1]
    width = out_ref.shape[1]
    got = got_ref[0:STEPS].reshape(STEPS * SLOTS, width)
    out_ref[...] = (total_ref[...] + dot(put_ref[...], got)).astype(jnp.bfloat16)

    @pl.when(me < STEPS)
    def _():
        out_ref[0:NB, :] = own_ref[pl.ds(jnp.minimum(me, STEPS - 1), 1)].reshape(NB, width)


def place(at, u, put, got, total):
    vmem = pl.BlockSpec(memory_space=pltpu.VMEM)
    return pl.pallas_call(
        place_kernel,
        out_shape=jax.ShapeDtypeStruct(total.shape, jnp.bfloat16),
        in_specs=[pl.BlockSpec(memory_space=pltpu.SMEM)] + [vmem] * 4,
        out_specs=vmem,
        compiler_params=pltpu.CompilerParams(vmem_limit_bytes=32 * 2**20),
        cost_estimate=pl.CostEstimate(
            flops=2 * total.size * STEPS * SLOTS, bytes_accessed=6 * 2**20, transcendentals=0
        ),
    )(at, u, put, got, total)


def body(matrix, panels, diag_blocks, pivots):
    width = matrix.shape[1]
    zh, x, y = lax.axis_index("zh"), lax.axis_index("x"), lax.axis_index("y")
    zl, c = lax.axis_index("zl"), lax.axis_index("c")
    at = jnp.stack([zh, x, zl, c]).astype(jnp.int32)
    me = zh * 4 + x
    local = me * ROWS + jnp.arange(ROWS, dtype=jnp.int32)
    t_ids = jnp.arange(STEPS, dtype=jnp.int32)
    i_ids = jnp.arange(NB, dtype=jnp.int32)

    wide, pivots, matrix = lax.optimization_barrier((jnp.broadcast_to(panels, (8,) + panels.shape), pivots, matrix))
    by_y = exchange(wide, "y")

    same = pivots[:, :, None, None] == pivots[None, None]
    before = (t_ids[None, :] < t_ids[:, None])[:, None, :, None]
    code = jnp.where(same & before, t_ids[:, None] * ROWS + i_ids[None, :], -1)
    origin = jnp.max(code, axis=(2, 3))
    base = jnp.where(origin >= 0, origin, pivots)

    picked = dot(picks(base.reshape(-1), local), matrix).astype(jnp.bfloat16)
    active = sum(dealt(picked.reshape(STEPS, 4, 64, width).transpose(1, 0, 2, 3), "x"))
    active = active.reshape(STEPS, 4, 16, width).transpose(1, 0, 2, 3)

    pair = jnp.array(PAIRS, jnp.int32).reshape(8, 2, 2)
    pair = lax.dynamic_index_in_dim(pair, y // 4, 1, keepdims=False)
    swapped_at = jnp.where(origin >= 0, origin // ROWS, -1)
    ids = jnp.where(swapped_at[None] > t_ids[:, None, None], origin[None], pivots[None])
    ids = lax.dynamic_slice_in_dim(ids.reshape(STEPS * STEPS, NB), y % 4 * 64, 64, 1)
    rows = l_rows(at, pair[:, 0], pair[:, 1], ids, by_y)

    across = shift(by_y, "zl", 1)
    high, low = inverses(diag_blocks)
    chunk = add_up(exchange(rows, ("zl", "c")))
    chunk = add_up(everyone(chunk, "x"))
    active, chunk, across, high, low, pivots = lax.optimization_barrier((active, chunk, across, high, low, pivots))
    both = jnp.concatenate([jnp.broadcast_to(chunk, (4,) + chunk.shape), active], axis=1)
    both = exchange(both, "zh")
    chunk, active = add_up(both[:, :4]), add_up(both[:, 4:])
    active = jnp.stack(passed(active, "zh"))
    chunk = everyone(chunk, "y")
    whole = [by_y, shift(by_y, "c", 1), across, shift(across, "c", 1)]
    active, chunk, whole[1], whole[3] = lax.optimization_barrier((active, chunk, whole[1], whole[3]))
    active = passed(active, "x")
    across = shift(chunk, "zl", 1)
    beside = shift(chunk, "c", 1)
    active[1], active[2], active[3], across = lax.optimization_barrier((*active[1:], across))
    blocks = [chunk, beside, across, shift(across, "c", 1)]

    same = pivots[:, :, None, None] == pivots[None, None]
    after = (t_ids[None, :] > t_ids[:, None])[:, None, :, None]
    stays = ~jnp.any(same & after, axis=(2, 3))
    owner = jnp.where(stays, pivots // ROWS, -1)
    ahead = (owner[:, :, None] == owner[:, None, :]) & (i_ids[None, :] < i_ids[:, None])
    rank = jnp.where(stays, jnp.sum(ahead, axis=2, dtype=jnp.int32), -1)
    rounds = (jnp.max(rank) + SLOTS) // SLOTS
    here = (pivots.reshape(-1)[None, :] == local[:, None]) & stays.reshape(-1)[None, :]
    tag = jnp.max(jnp.where(here, (t_ids[:, None] * NB + rank).reshape(-1)[None, :], -1), axis=1)
    last = jnp.where(tag >= 0, tag // NB, -1)
    at_rank = jnp.where(tag >= 0, tag % NB, -1)
    mine = jnp.minimum(me, STEPS - 1)
    my_rank = jnp.where(me < STEPS, lax.dynamic_index_in_dim(rank, mine, 0, keepdims=False), -1)
    my_owner = lax.dynamic_index_in_dim(owner, mine, 0, keepdims=False)

    def slots(q):
        n = my_rank - q * SLOTS
        return jnp.where((n >= 0) & (n < SLOTS), my_owner * SLOTS + n, -1)

    def landing(q):
        n = at_rank - q * SLOTS
        return picks(jnp.where((n >= 0) & (n < SLOTS), last * SLOTS + n, -1), jnp.arange(STEPS * SLOTS, dtype=jnp.int32))

    def deliver(sent):
        return exchange(sent.reshape(16, SLOTS, width), ("zh", "x"))

    u, old, send = solve(at, slots(0)[None], high, low, matrix[:NB], active, blocks, whole)
    total = update(at, jnp.broadcast_to(last[:, None], (ROWS, 128)), u, matrix, whole)
    got = deliver(send)
    total, got = lax.optimization_barrier((total, got))

    def more(state):
        q, total = state
        sent = dot(picks(jnp.arange(16 * SLOTS, dtype=jnp.int32), slots(q)), old).astype(jnp.bfloat16)
        got = deliver(sent)[:STEPS].reshape(STEPS * SLOTS, width)
        return q + 1, total + dot(landing(q), got)

    _, total = lax.while_loop(lambda state: state[0] < rounds, more, (jnp.int32(1), total))
    return place(at, u, landing(0), got, total)


def solution(mesh):
    fine = Mesh(mesh.devices.reshape(4, 4, 8, 2, 2), FINE)
    prow, pcol = ("zh", "x"), ("y", "zl", "c")
    return jax.shard_map(
        body,
        mesh=fine,
        in_specs=(P(prow, pcol), P(None, prow + pcol, None), P(), P()),
        out_specs=P(prow, pcol),
        check_vma=False,
    )
```

```python
import jax
import jax.numpy as jnp
from jax import lax
from jax.experimental import pallas as pl
from jax.experimental.pallas import tpu as pltpu
from jax.sharding import Mesh
from jax.sharding import PartitionSpec as P

STEPS = 6
NB = 256
ROWS = 1024
FINE = ("zh", "x", "y", "zl", "c")
PAIRS = [(s, k) for k in range(STEPS) for s in range(k + 1, STEPS)] + [(0, 0)]
PLACE = {pair: n for n, pair in enumerate(PAIRS)}
SLOTS = 32


def split(v):
    high = v.astype(jnp.bfloat16)
    return high, (v - high.astype(jnp.float32)).astype(jnp.bfloat16)


def dot(a, b):
    return jnp.dot(a, b, preferred_element_type=jnp.float32)


def dot3(a, b):
    ah, al = split(a)
    bh, bl = split(b)
    return dot(ah, bh) + (dot(ah, bl) + dot(al, bh))


def inverse_kernel(l_ref, high_ref, low_ref):
    row = lax.broadcasted_iota(jnp.int32, (NB, NB), 0)
    col = lax.broadcasted_iota(jnp.int32, (NB, NB), 1)
    eye = (row == col).astype(jnp.float32)
    lower = [l_ref[s] for s in range(STEPS)]
    inv = [eye] * STEPS
    size = 1
    while size < NB:
        joins = (row // (2 * size) == col // (2 * size)) & (row // size > col // size)
        parts = [jnp.where(joins, m, 0.0) for m in lower]
        if size == 1:
            inv = [eye - m for m in parts]
        else:
            left = [dot3(m, x) for m, x in zip(parts, inv)]
            inv = [x - dot3(x, m) for x, m in zip(inv, left)]
        size *= 2
    for s in range(STEPS):
        high_ref[s], low_ref[s] = split(inv[s])


def inverses(diag_blocks):
    out = jax.ShapeDtypeStruct((STEPS, NB, NB), jnp.bfloat16)
    spec = pl.BlockSpec(memory_space=pltpu.VMEM)
    return pl.pallas_call(
        inverse_kernel,
        out_shape=(out, out),
        in_specs=[spec],
        out_specs=(spec, spec),
        compiler_params=pltpu.CompilerParams(vmem_limit_bytes=48 * 2**20),
        cost_estimate=pl.CostEstimate(flops=2 * 42 * 6 * NB**3, bytes_accessed=3 * 2**20, transcendentals=0),
    )(diag_blocks)


def exchange(v, axis):
    return lax.all_to_all(v, axis, 0, 0)


def everyone(v, axis):
    n = lax.axis_size(axis)
    return exchange(jnp.broadcast_to(v[None], (n,) + v.shape), axis)


def add_up(v):
    return jnp.sum(v.astype(jnp.float32), axis=0).astype(v.dtype)


def shift(v, axis, by):
    n = lax.axis_size(axis)
    return lax.ppermute(v, axis, [(i, (i + by) % n) for i in range(n)])


def dealt(v, axis):
    n, at = lax.axis_size(axis), lax.axis_index(axis)
    parts = [lax.dynamic_index_in_dim(v, (at + d) % n, 0, keepdims=False) for d in range(n)]
    return parts[:1] + [shift(parts[d], axis, d) for d in range(1, n)]


def passed(v, axis):
    return [v] + [shift(v, axis, d) for d in range(1, lax.axis_size(axis))]


def picks(ids, held):
    return (ids[:, None] == held[None, :]).astype(jnp.bfloat16)


def l_rows_kernel(at_ref, ts_ref, ks_ref, ids_ref, panels_ref, out_ref):
    zh, x, zl, c = at_ref[0], at_ref[1], at_ref[2], at_ref[3]
    lane = lax.broadcasted_iota(jnp.int32, (NB, 64), 0)
    held = (zh * 4 + x) * ROWS + zl * 64 + c * 32 + lane // 32 * 128 + lane % 32
    for m in range(8):
        t, k = ts_ref[m], ks_ref[m]
        put = jnp.where(held == ids_ref[pl.ds(k * STEPS + t, 1), :], 1.0, 0.0).astype(jnp.bfloat16)
        mine = panels_ref[:, pl.ds(k, 1)].reshape(NB, NB)
        rows = lax.dot_general(put, mine, (((0,), (0,)), ((), ())), preferred_element_type=jnp.float32)
        out_ref[:, m // 2, :, m % 2 * NB : m % 2 * NB + NB] = rows.astype(jnp.bfloat16).reshape(4, 16, NB)


def l_rows(at, ts, ks, ids, panels):
    vmem, smem = pl.BlockSpec(memory_space=pltpu.VMEM), pl.BlockSpec(memory_space=pltpu.SMEM)
    return pl.pallas_call(
        l_rows_kernel,
        out_shape=jax.ShapeDtypeStruct((4, 4, 16, 2 * NB), jnp.bfloat16),
        in_specs=[smem, smem, smem, vmem, vmem],
        out_specs=vmem,
        compiler_params=pltpu.CompilerParams(vmem_limit_bytes=16 * 2**20),
        cost_estimate=pl.CostEstimate(flops=2 * 8 * 64 * NB * NB, bytes_accessed=2**20, transcendentals=0),
    )(at, ts, ks, ids, panels)


def turned(zl, c, n):
    return lax.rem(zl + n // 2, 2), lax.rem(c + n % 2, 2)


def solve_kernel(at_ref, slot_ref, high_ref, low_ref, matrix_ref, *refs):
    active_in, blocks_in, panels_in = refs[:4], refs[4:6], refs[6:10]
    u_ref, old_ref, send_ref, active, blocks, panels, active_sem, blocks_sem, panels_sem = refs[10:]
    zh, x, zl, c = at_ref[0], at_ref[1], at_ref[2], at_ref[3]
    me = zh * 4 + x
    width = matrix_ref.shape[1]
    copies = []
    for d in range(4):
        for e in range(4):
            target = active.at[lax.rem(x - d + 4, 4), lax.rem(zh - e + 4, 4)]
            copies.append(pltpu.make_async_copy(active_in[d].at[e], target, active_sem.at[d * 4 + e]))
    for n in range(2):
        target = blocks.at[:, :, lax.rem(c + n, 2)]
        copies.append(pltpu.make_async_copy(blocks_in[n], target, blocks_sem.at[n]))
    for n in range(4):
        a, b = turned(zl, c, n)
        copies.append(pltpu.make_async_copy(panels_in[n].at[0:2], panels.at[:, a, b], panels_sem.at[n]))
    for copy in copies:
        copy.start()
    for copy in copies[:16]:
        copy.wait()

    def rows_of(n):
        return active[:, :, n].reshape(NB, width)

    old_ref[...] = matrix_ref[0:NB, :]
    for s in range(STEPS):
        top = rows_of(s)
        u = (dot(high_ref[s], top) + dot(low_ref[s], top)).astype(jnp.bfloat16)
        u_ref[s] = u

        if s == 0:
            for copy in copies[16:]:
                copy.wait()
        for t in range(s + 1, STEPS):
            n = PLACE[(t, s)]
            left = n // 2 % 2 * NB
            block = blocks[n % 2 * 4 : n % 2 * 4 + 4, :, :, n // 4, :, left : left + NB].reshape(NB, NB)
            less = rows_of(t).astype(jnp.float32) - dot(block, u)
            active[:, :, t] = less.astype(jnp.bfloat16).reshape(4, 4, 16, width)

    for s in range(STEPS - 1):

        @pl.when((s < me) & (me < STEPS))
        def _():
            panel = panels[:, :, :, s].reshape(NB, NB)
            old_ref[...] = (old_ref[...].astype(jnp.float32) - dot(panel, u_ref[s])).astype(jnp.bfloat16)

    slot = lax.broadcasted_iota(jnp.int32, (16 * SLOTS, NB), 0)
    put = jnp.where(slot == slot_ref[...], 1.0, 0.0).astype(jnp.bfloat16)
    send_ref[...] = dot(put, old_ref[...]).astype(jnp.bfloat16)


def solve(at, slot, high, low, matrix, active, blocks, panels):
    width = matrix.shape[1]
    vmem, anywhere = pl.BlockSpec(memory_space=pltpu.VMEM), pl.BlockSpec(memory_space=pl.ANY)
    return pl.pallas_call(
        solve_kernel,
        out_shape=(
            jax.ShapeDtypeStruct((STEPS, NB, width), jnp.bfloat16),
            jax.ShapeDtypeStruct((NB, width), jnp.bfloat16),
            jax.ShapeDtypeStruct((16 * SLOTS, width), jnp.bfloat16),
        ),
        in_specs=[pl.BlockSpec(memory_space=pltpu.SMEM)] + [vmem] * 4 + [anywhere] * 10,
        out_specs=(vmem,) * 3,
        scratch_shapes=[
            pltpu.VMEM((4, 4, STEPS, 16, width), jnp.bfloat16),
            pltpu.VMEM((8, 2, 2, 4, 16, 2 * NB), jnp.bfloat16),
            pltpu.VMEM((2, 2, 2, STEPS, 32, NB), jnp.bfloat16),
            pltpu.SemaphoreType.DMA((16,)),
            pltpu.SemaphoreType.DMA((2,)),
            pltpu.SemaphoreType.DMA((4,)),
        ],
        compiler_params=pltpu.CompilerParams(vmem_limit_bytes=58 * 2**20),
        cost_estimate=pl.CostEstimate(flops=2 * 35 * NB * NB * width, bytes_accessed=9 * 2**20, transcendentals=0),
    )(at, slot, high, low, matrix, *active, *blocks, *panels)


def update_kernel(at_ref, last_ref, u_ref, matrix_ref, *refs):
    panels_in, (out_ref, panels, panels_sem) = refs[:4], refs[4:]
    zl, c = at_ref[2], at_ref[3]
    width = matrix_ref.shape[1]
    copies = []
    for n in range(4):
        a, b = turned(zl, c, n)
        copies.append(pltpu.make_async_copy(panels_in[n], panels.at[:, a, b], panels_sem.at[n]))
    for copy in copies:
        copy.start()
    for copy in copies:
        copy.wait()
    tall = 256

    @pl.loop(0, ROWS // tall)
    def _(i):
        span = pl.ds(pl.multiple_of(i * tall, tall), tall)
        last = jnp.concatenate([last_ref[span, :]] * (width // 128), axis=1)
        rows = matrix_ref[span, :].astype(jnp.float32)
        for s in range(STEPS):
            panel = panels[pl.ds(i * (tall // 128), tall // 128), :, :, s].reshape(tall, NB)
            rows = jnp.where(last == s, 0.0, rows) - dot(panel, u_ref[s])
            rows = jnp.where(last >= 0, rows, rows.astype(jnp.bfloat16).astype(jnp.float32))
        out_ref[span, :] = rows

    me = at_ref[0] * 4 + at_ref[1]

    @pl.when(me < STEPS)
    def _():
        own = u_ref[pl.ds(jnp.minimum(me, STEPS - 1), 1)].reshape(NB, width)
        out_ref[0:NB, :] = own.astype(jnp.float32)


def update(at, last, u, matrix, panels):
    vmem, anywhere = pl.BlockSpec(memory_space=pltpu.VMEM), pl.BlockSpec(memory_space=pl.ANY)
    return pl.pallas_call(
        update_kernel,
        out_shape=jax.ShapeDtypeStruct(matrix.shape, jnp.float32),
        in_specs=[pl.BlockSpec(memory_space=pltpu.SMEM)] + [vmem] * 3 + [anywhere] * 4,
        out_specs=vmem,
        scratch_shapes=[pltpu.VMEM((8, 2, 2, STEPS, 32, NB), jnp.bfloat16), pltpu.SemaphoreType.DMA((4,))],
        compiler_params=pltpu.CompilerParams(vmem_limit_bytes=58 * 2**20),
        cost_estimate=pl.CostEstimate(
            flops=2 * matrix.size * STEPS * NB, bytes_accessed=8 * 2**20, transcendentals=0
        ),
    )(at, last, u, matrix, *panels)


def place_kernel(put_ref, got_ref, total_ref, out_ref):
    width = out_ref.shape[1]
    got = got_ref[0:STEPS].reshape(STEPS * SLOTS, width)
    out_ref[...] = (total_ref[...] + dot(put_ref[...], got)).astype(jnp.bfloat16)


def place(put, got, total):
    vmem = pl.BlockSpec(memory_space=pltpu.VMEM)
    return pl.pallas_call(
        place_kernel,
        out_shape=jax.ShapeDtypeStruct(total.shape, jnp.bfloat16),
        in_specs=[vmem] * 3,
        out_specs=vmem,
        compiler_params=pltpu.CompilerParams(vmem_limit_bytes=32 * 2**20),
        cost_estimate=pl.CostEstimate(
            flops=2 * total.size * STEPS * SLOTS, bytes_accessed=6 * 2**20, transcendentals=0
        ),
    )(put, got, total)


def origin_kernel(pivots_ref, origin_ref, base_ref):
    rows = pivots_ref[...]
    columns = jnp.transpose(jnp.concatenate([rows, rows[: 8 - STEPS]], axis=0))
    index = lax.broadcasted_iota(jnp.int32, (NB, NB), 0).astype(jnp.float32)
    for s in range(STEPS):
        row = rows[s : s + 1]
        latest = jnp.full((1, NB), -1.0, jnp.float32)
        for t in range(s):
            code = jnp.where(columns[:, t : t + 1] == row, index + float(t * ROWS), -1.0)
            latest = jnp.maximum(latest, jnp.max(code, axis=0, keepdims=True))
        latest = latest.astype(jnp.int32)
        origin_ref[s : s + 1, :] = latest
        base_ref[s : s + 1, :] = jnp.where(latest >= 0, latest, row)


def origins(pivots):
    vmem = pl.BlockSpec(memory_space=pltpu.VMEM)
    out = jax.ShapeDtypeStruct(pivots.shape, jnp.int32)
    return pl.pallas_call(
        origin_kernel,
        out_shape=(out, out),
        in_specs=[vmem],
        out_specs=(vmem, vmem),
        compiler_params=pltpu.CompilerParams(vmem_limit_bytes=16 * 2**20),
        cost_estimate=pl.CostEstimate(flops=1000, bytes_accessed=20000, transcendentals=0),
    )(pivots)


def body(matrix, panels, diag_blocks, pivots):
    width = matrix.shape[1]
    zh, x, y = lax.axis_index("zh"), lax.axis_index("x"), lax.axis_index("y")
    zl, c = lax.axis_index("zl"), lax.axis_index("c")
    at = jnp.stack([zh, x, zl, c]).astype(jnp.int32)
    me = zh * 4 + x
    local = me * ROWS + jnp.arange(ROWS, dtype=jnp.int32)
    t_ids = jnp.arange(STEPS, dtype=jnp.int32)
    i_ids = jnp.arange(NB, dtype=jnp.int32)

    wide, pivots, matrix = lax.optimization_barrier((jnp.broadcast_to(panels, (8,) + panels.shape), pivots, matrix))
    by_y = exchange(wide, "y")

    origin, base = origins(pivots)

    picked = dot(picks(base.reshape(-1), local), matrix).astype(jnp.bfloat16)
    active = sum(dealt(picked.reshape(STEPS, 4, 64, width).transpose(1, 0, 2, 3), "x"))
    active = active.reshape(STEPS, 4, 16, width).transpose(1, 0, 2, 3)

    pair = jnp.array(PAIRS, jnp.int32).reshape(8, 2, 2)
    pair = lax.dynamic_index_in_dim(pair, y // 4, 1, keepdims=False)
    swapped_at = jnp.where(origin >= 0, origin // ROWS, -1)
    ids = jnp.where(swapped_at[None] > t_ids[:, None, None], origin[None], pivots[None])
    ids = lax.dynamic_slice_in_dim(ids.reshape(STEPS * STEPS, NB), y % 4 * 64, 64, 1)
    rows = l_rows(at, pair[:, 0], pair[:, 1], ids, by_y)

    chunk = add_up(exchange(rows, ("zl", "c")))
    both = jnp.concatenate([jnp.broadcast_to(chunk, (4,) + chunk.shape), active], axis=1)
    both, pivots, diag_blocks = lax.optimization_barrier((both, pivots, diag_blocks))
    high, low = inverses(diag_blocks)
    both = exchange(both, "zh")
    chunk = add_up(both[:, :4])
    wide = jnp.broadcast_to(chunk, (4,) + chunk.shape)
    wide, both, high, low = lax.optimization_barrier((wide, both, high, low))
    active = add_up(both[:, 4:])
    chunk = add_up(exchange(wide, "x"))
    active = jnp.stack(passed(active, "zh"))
    panels_across = shift(by_y, "zl", 1)
    active, chunk, panels_across = lax.optimization_barrier((active, chunk, panels_across))
    active = passed(active, "x")
    chunk = everyone(chunk, ("y", "zl")).reshape(8, 2, 4, 16, 2 * NB)
    whole = [by_y, shift(by_y, "c", 1), panels_across, shift(panels_across, "c", 1)]
    active[1], pivots = lax.optimization_barrier((active[1], pivots))

    same = pivots[:, :, None, None] == pivots[None, None]
    after = (t_ids[None, :] > t_ids[:, None])[:, None, :, None]
    stays = ~jnp.any(same & after, axis=(2, 3))
    owner = jnp.where(stays, pivots // ROWS, -1)
    ahead = (owner[:, :, None] == owner[:, None, :]) & (i_ids[None, :] < i_ids[:, None])
    rank = jnp.where(stays, jnp.sum(ahead, axis=2, dtype=jnp.int32), -1)
    rounds = (jnp.max(rank) + SLOTS) // SLOTS
    mine = jnp.minimum(me, STEPS - 1)
    my_rank = jnp.where(me < STEPS, lax.dynamic_index_in_dim(rank, mine, 0, keepdims=False), -1)
    my_owner = lax.dynamic_index_in_dim(owner, mine, 0, keepdims=False)

    def slots(q):
        n = my_rank - q * SLOTS
        return jnp.where((n >= 0) & (n < SLOTS), my_owner * SLOTS + n, -1)

    first = slots(0)[None]
    active[2], active[3], chunk, whole[1], whole[3], first = lax.optimization_barrier(
        (*active[2:], chunk, whole[1], whole[3], first)
    )
    blocks = [chunk, shift(chunk, "c", 1)]
    u, old, send = solve(at, first, high, low, matrix, active, blocks, whole)

    got = exchange(send.reshape(16, SLOTS, width), ("zh", "x"))
    u, pivots = lax.optimization_barrier((u, pivots))
    here = (pivots.reshape(-1)[None, :] == local[:, None]) & stays.reshape(-1)[None, :]
    tag = jnp.max(jnp.where(here, (t_ids[:, None] * NB + rank).reshape(-1)[None, :], -1), axis=1)
    last = jnp.where(tag >= 0, tag // NB, -1)
    at_rank = jnp.where(tag >= 0, tag % NB, -1)

    def landing(q):
        n = at_rank - q * SLOTS
        return picks(jnp.where((n >= 0) & (n < SLOTS), last * SLOTS + n, -1), jnp.arange(STEPS * SLOTS, dtype=jnp.int32))

    def deliver(sent):
        return exchange(sent.reshape(16, SLOTS, width), ("zh", "x"))

    total = update(at, jnp.broadcast_to(last[:, None], (ROWS, 128)), u, matrix, whole)
    total, got = lax.optimization_barrier((total, got))

    def more(state):
        q, total = state
        sent = dot(picks(jnp.arange(16 * SLOTS, dtype=jnp.int32), slots(q)), old).astype(jnp.bfloat16)
        got = deliver(sent)[:STEPS].reshape(STEPS * SLOTS, width)
        return q + 1, total + dot(landing(q), got)

    _, total = lax.while_loop(lambda state: state[0] < rounds, more, (jnp.int32(1), total))
    return place(landing(0), got, total)


def solution(mesh):
    fine = Mesh(mesh.devices.reshape(4, 4, 8, 2, 2), FINE)
    prow, pcol = ("zh", "x"), ("y", "zl", "c")
    return jax.shard_map(
        body,
        mesh=fine,
        in_specs=(P(prow, pcol), P(None, prow + pcol, None), P(), P()),
        out_specs=P(prow, pcol),
        check_vma=False,
    )
```

```python
import jax
import jax.numpy as jnp
from jax import lax
from jax.experimental import pallas as pl
from jax.experimental.pallas import tpu as pltpu
from jax.sharding import Mesh
from jax.sharding import PartitionSpec as P

STEPS = 6
NB = 256
ROWS = 1024
FINE = ("zh", "x", "y", "zl", "c")
PAIRS = [(s, k) for k in range(STEPS) for s in range(k + 1, STEPS)] + [(0, 0)]
PLACE = {pair: n for n, pair in enumerate(PAIRS)}
CAP = 144
SLOTS = 32


def split(v):
    high = v.astype(jnp.bfloat16)
    return high, (v - high.astype(jnp.float32)).astype(jnp.bfloat16)


def dot(a, b):
    return jnp.dot(a, b, preferred_element_type=jnp.float32)


def dot3(a, b):
    ah, al = split(a)
    bh, bl = split(b)
    return dot(ah, bh) + (dot(ah, bl) + dot(al, bh))


def inverse_kernel(l_ref, high_ref, low_ref):
    row = lax.broadcasted_iota(jnp.int32, (NB, NB), 0)
    col = lax.broadcasted_iota(jnp.int32, (NB, NB), 1)
    eye = (row == col).astype(jnp.float32)
    lower = [l_ref[s] for s in range(STEPS)]
    inv = [eye] * STEPS
    size = 1
    while size < NB:
        joins = (row // (2 * size) == col // (2 * size)) & (row // size > col // size)
        parts = [jnp.where(joins, m, 0.0) for m in lower]
        if size == 1:
            inv = [eye - m for m in parts]
        else:
            left = [dot3(m, x) for m, x in zip(parts, inv)]
            inv = [x - dot3(x, m) for x, m in zip(inv, left)]
        size *= 2
    for s in range(STEPS):
        high_ref[s], low_ref[s] = split(inv[s])


def inverses(diag_blocks):
    out = jax.ShapeDtypeStruct((STEPS, NB, NB), jnp.bfloat16)
    spec = pl.BlockSpec(memory_space=pltpu.VMEM)
    return pl.pallas_call(
        inverse_kernel,
        out_shape=(out, out),
        in_specs=[spec],
        out_specs=(spec, spec),
        compiler_params=pltpu.CompilerParams(vmem_limit_bytes=48 * 2**20),
        cost_estimate=pl.CostEstimate(flops=2 * 42 * 6 * NB**3, bytes_accessed=3 * 2**20, transcendentals=0),
    )(diag_blocks)


def exchange(v, axis):
    return lax.all_to_all(v, axis, 0, 0)


def everyone(v, axis):
    n = lax.axis_size(axis)
    return exchange(jnp.broadcast_to(v[None], (n,) + v.shape), axis)


def add_up(v):
    return jnp.sum(v.astype(jnp.float32), axis=0).astype(v.dtype)


def shift(v, axis, by):
    n = lax.axis_size(axis)
    return lax.ppermute(v, axis, [(i, (i + by) % n) for i in range(n)])


def dealt(v, axis):
    n, at = lax.axis_size(axis), lax.axis_index(axis)
    parts = [lax.dynamic_index_in_dim(v, (at + d) % n, 0, keepdims=False) for d in range(n)]
    return parts[:1] + [shift(parts[d], axis, d) for d in range(1, n)]


def passed(v, axis):
    return [v] + [shift(v, axis, d) for d in range(1, lax.axis_size(axis))]


def picks(ids, held):
    return (ids[:, None] == held[None, :]).astype(jnp.bfloat16)


def l_rows_kernel(at_ref, ts_ref, ks_ref, ids_ref, panels_ref, out_ref):
    zh, x, zl, c = at_ref[0], at_ref[1], at_ref[2], at_ref[3]
    lane = lax.broadcasted_iota(jnp.int32, (NB, 64), 0)
    held = (zh * 4 + x) * ROWS + zl * 64 + c * 32 + lane // 32 * 128 + lane % 32
    for m in range(8):
        t, k = ts_ref[m], ks_ref[m]
        put = jnp.where(held == ids_ref[pl.ds(k * STEPS + t, 1), :], 1.0, 0.0).astype(jnp.bfloat16)
        mine = panels_ref[:, pl.ds(k, 1)].reshape(NB, NB)
        rows = lax.dot_general(put, mine, (((0,), (0,)), ((), ())), preferred_element_type=jnp.float32)
        out_ref[:, m // 2, :, m % 2 * NB : m % 2 * NB + NB] = rows.astype(jnp.bfloat16).reshape(4, 16, NB)


def l_rows(at, ts, ks, ids, panels):
    vmem, smem = pl.BlockSpec(memory_space=pltpu.VMEM), pl.BlockSpec(memory_space=pltpu.SMEM)
    return pl.pallas_call(
        l_rows_kernel,
        out_shape=jax.ShapeDtypeStruct((4, 4, 16, 2 * NB), jnp.bfloat16),
        in_specs=[smem, smem, smem, vmem, vmem],
        out_specs=vmem,
        compiler_params=pltpu.CompilerParams(vmem_limit_bytes=16 * 2**20),
        cost_estimate=pl.CostEstimate(flops=2 * 8 * 64 * NB * NB, bytes_accessed=2**20, transcendentals=0),
    )(at, ts, ks, ids, panels)


def turned(zl, c, n):
    return lax.rem(zl + n // 2, 2), lax.rem(c + n % 2, 2)


def solve_kernel(at_ref, slot_ref, high_ref, low_ref, matrix_ref, *refs):
    active_in, blocks_in, panels_in = refs[0], refs[1:3], refs[3:7]
    u_ref, old_ref, send_ref, active, blocks, panels, active_sem, blocks_sem, panels_sem = refs[7:]
    zh, x, zl, c = at_ref[0], at_ref[1], at_ref[2], at_ref[3]
    me = zh * 4 + x
    width = matrix_ref.shape[1]
    copies = [pltpu.make_async_copy(active_in, active, active_sem.at[0])]
    for n in range(2):
        target = blocks.at[:, :, lax.rem(c + n, 2)]
        copies.append(pltpu.make_async_copy(blocks_in[n], target, blocks_sem.at[n]))
    for n in range(4):
        a, b = turned(zl, c, n)
        copies.append(pltpu.make_async_copy(panels_in[n].at[0:2], panels.at[:, a, b], panels_sem.at[n]))
    for copy in copies:
        copy.start()
    for copy in copies[:1]:
        copy.wait()

    def rows_of(n):
        return active[n]

    old_ref[...] = matrix_ref[0:NB, :]
    for s in range(STEPS):
        top = rows_of(s)
        u = (dot(high_ref[s], top) + dot(low_ref[s], top)).astype(jnp.bfloat16)
        u_ref[s] = u

        if s == 0:
            for copy in copies[1:]:
                copy.wait()
        for t in range(s + 1, STEPS):
            n = PLACE[(t, s)]
            left = n // 2 % 2 * NB
            block = blocks[n % 2 * 4 : n % 2 * 4 + 4, :, :, n // 4, :, left : left + NB].reshape(NB, NB)
            less = rows_of(t).astype(jnp.float32) - dot(block, u)
            active[t] = less.astype(jnp.bfloat16)

    for s in range(STEPS - 1):

        @pl.when((s < me) & (me < STEPS))
        def _():
            panel = panels[:, :, :, s].reshape(NB, NB)
            old_ref[...] = (old_ref[...].astype(jnp.float32) - dot(panel, u_ref[s])).astype(jnp.bfloat16)

    slot = lax.broadcasted_iota(jnp.int32, (16 * SLOTS, NB), 0)
    put = jnp.where(slot == slot_ref[...], 1.0, 0.0).astype(jnp.bfloat16)
    send_ref[...] = dot(put, old_ref[...]).astype(jnp.bfloat16)


def solve(at, slot, high, low, matrix, active, blocks, panels):
    width = matrix.shape[1]
    vmem, anywhere = pl.BlockSpec(memory_space=pltpu.VMEM), pl.BlockSpec(memory_space=pl.ANY)
    return pl.pallas_call(
        solve_kernel,
        out_shape=(
            jax.ShapeDtypeStruct((STEPS, NB, width), jnp.bfloat16),
            jax.ShapeDtypeStruct((NB, width), jnp.bfloat16),
            jax.ShapeDtypeStruct((16 * SLOTS, width), jnp.bfloat16),
        ),
        in_specs=[pl.BlockSpec(memory_space=pltpu.SMEM)] + [vmem] * 4 + [anywhere] * 7,
        out_specs=(vmem,) * 3,
        scratch_shapes=[
            pltpu.VMEM((STEPS, NB, width), jnp.bfloat16),
            pltpu.VMEM((8, 2, 2, 4, 16, 2 * NB), jnp.bfloat16),
            pltpu.VMEM((2, 2, 2, STEPS, 32, NB), jnp.bfloat16),
            pltpu.SemaphoreType.DMA((1,)),
            pltpu.SemaphoreType.DMA((2,)),
            pltpu.SemaphoreType.DMA((4,)),
        ],
        compiler_params=pltpu.CompilerParams(vmem_limit_bytes=58 * 2**20),
        cost_estimate=pl.CostEstimate(flops=2 * 35 * NB * NB * width, bytes_accessed=9 * 2**20, transcendentals=0),
    )(at, slot, high, low, matrix, active, *blocks, *panels)


def update_kernel(at_ref, last_ref, u_ref, matrix_ref, *refs):
    panels_in, (out_ref, panels, panels_sem) = refs[:4], refs[4:]
    zl, c = at_ref[2], at_ref[3]
    width = matrix_ref.shape[1]
    copies = []
    for n in range(4):
        a, b = turned(zl, c, n)
        copies.append(pltpu.make_async_copy(panels_in[n], panels.at[:, a, b], panels_sem.at[n]))
    for copy in copies:
        copy.start()
    for copy in copies:
        copy.wait()
    tall = 256

    @pl.loop(0, ROWS // tall)
    def _(i):
        span = pl.ds(pl.multiple_of(i * tall, tall), tall)
        last = jnp.concatenate([last_ref[span, :]] * (width // 128), axis=1)
        rows = matrix_ref[span, :].astype(jnp.float32)
        for s in range(STEPS):
            panel = panels[pl.ds(i * (tall // 128), tall // 128), :, :, s].reshape(tall, NB)
            rows = jnp.where(last == s, 0.0, rows) - dot(panel, u_ref[s])
            rows = jnp.where(last >= 0, rows, rows.astype(jnp.bfloat16).astype(jnp.float32))
        out_ref[span, :] = rows

    me = at_ref[0] * 4 + at_ref[1]

    @pl.when(me < STEPS)
    def _():
        own = u_ref[pl.ds(jnp.minimum(me, STEPS - 1), 1)].reshape(NB, width)
        out_ref[0:NB, :] = own.astype(jnp.float32)


def update(at, last, u, matrix, panels):
    vmem, anywhere = pl.BlockSpec(memory_space=pltpu.VMEM), pl.BlockSpec(memory_space=pl.ANY)
    return pl.pallas_call(
        update_kernel,
        out_shape=jax.ShapeDtypeStruct(matrix.shape, jnp.float32),
        in_specs=[pl.BlockSpec(memory_space=pltpu.SMEM)] + [vmem] * 3 + [anywhere] * 4,
        out_specs=vmem,
        scratch_shapes=[pltpu.VMEM((8, 2, 2, STEPS, 32, NB), jnp.bfloat16), pltpu.SemaphoreType.DMA((4,))],
        compiler_params=pltpu.CompilerParams(vmem_limit_bytes=58 * 2**20),
        cost_estimate=pl.CostEstimate(
            flops=2 * matrix.size * STEPS * NB, bytes_accessed=8 * 2**20, transcendentals=0
        ),
    )(at, last, u, matrix, *panels)


def place_kernel(put_ref, got_ref, total_ref, out_ref):
    width = out_ref.shape[1]
    got = got_ref[0:STEPS].reshape(STEPS * SLOTS, width)
    out_ref[...] = (total_ref[...] + dot(put_ref[...], got)).astype(jnp.bfloat16)


def place(put, got, total):
    vmem = pl.BlockSpec(memory_space=pltpu.VMEM)
    return pl.pallas_call(
        place_kernel,
        out_shape=jax.ShapeDtypeStruct(total.shape, jnp.bfloat16),
        in_specs=[vmem] * 3,
        out_specs=vmem,
        compiler_params=pltpu.CompilerParams(vmem_limit_bytes=32 * 2**20),
        cost_estimate=pl.CostEstimate(
            flops=2 * total.size * STEPS * SLOTS, bytes_accessed=6 * 2**20, transcendentals=0
        ),
    )(put, got, total)


def origin_kernel(pivots_ref, origin_ref, base_ref, rank_ref):
    rows = pivots_ref[...]
    columns = jnp.transpose(jnp.concatenate([rows, rows[: 8 - STEPS]], axis=0))
    down = lax.broadcasted_iota(jnp.int32, (NB, NB), 0)
    index = down.astype(jnp.float32)
    earlier = jnp.where(down < lax.broadcasted_iota(jnp.int32, (NB, NB), 1), 1.0, 0.0).astype(jnp.bfloat16)
    prow = lax.broadcasted_iota(jnp.int32, (16, NB), 0)
    so_far = jnp.zeros((16, 1), jnp.float32)
    for s in range(STEPS):
        row = rows[s : s + 1]
        latest = jnp.full((1, NB), -1.0, jnp.float32)
        for t in range(s):
            code = jnp.where(columns[:, t : t + 1] == row, index + float(t * ROWS), -1.0)
            latest = jnp.maximum(latest, jnp.max(code, axis=0, keepdims=True))
        latest = latest.astype(jnp.int32)
        base = jnp.where(latest >= 0, latest, row)
        origin_ref[s : s + 1, :] = latest
        base_ref[s : s + 1, :] = base
        holds = jnp.where(prow == base // ROWS, 1.0, 0.0)
        ahead = dot(holds.astype(jnp.bfloat16), earlier) + so_far
        rank_ref[s : s + 1, :] = jnp.sum(holds * ahead, axis=0, keepdims=True).astype(jnp.int32)
        so_far = so_far + jnp.sum(holds, axis=1, keepdims=True)


def origins(pivots):
    vmem = pl.BlockSpec(memory_space=pltpu.VMEM)
    out = jax.ShapeDtypeStruct(pivots.shape, jnp.int32)
    return pl.pallas_call(
        origin_kernel,
        out_shape=(out,) * 3,
        in_specs=[vmem],
        out_specs=(vmem,) * 3,
        compiler_params=pltpu.CompilerParams(vmem_limit_bytes=16 * 2**20),
        cost_estimate=pl.CostEstimate(flops=1000, bytes_accessed=20000, transcendentals=0),
    )(pivots)


def pack_kernel(at_ref, base_ref, rank_ref, matrix_ref, out_ref):
    me, skip = at_ref[0], at_ref[1]
    slot = lax.broadcasted_iota(jnp.int32, (CAP, NB), 0)
    ids = jnp.zeros((CAP, 1), jnp.float32)
    for s in range(STEPS):
        base = base_ref[s : s + 1, :]
        code = jnp.where(base // ROWS == me, rank_ref[s : s + 1, :] - skip, -1)
        ids = ids + jnp.sum(jnp.where(slot == code, (base + 1).astype(jnp.float32), 0.0), axis=1, keepdims=True)
    local = ids.astype(jnp.int32) - 1 - me * ROWS
    put = jnp.where(lax.broadcasted_iota(jnp.int32, (CAP, ROWS), 1) == local, 1.0, 0.0).astype(jnp.bfloat16)
    out_ref[...] = dot(put, matrix_ref[...]).astype(jnp.bfloat16)


def pack(me, skip, base, rank, matrix):
    vmem = pl.BlockSpec(memory_space=pltpu.VMEM)
    return pl.pallas_call(
        pack_kernel,
        out_shape=jax.ShapeDtypeStruct((CAP, matrix.shape[1]), jnp.bfloat16),
        in_specs=[pl.BlockSpec(memory_space=pltpu.SMEM)] + [vmem] * 3,
        out_specs=vmem,
        compiler_params=pltpu.CompilerParams(vmem_limit_bytes=16 * 2**20),
        cost_estimate=pl.CostEstimate(flops=2 * CAP * matrix.size, bytes_accessed=2**20, transcendentals=0),
    )(jnp.stack([me, skip]).astype(jnp.int32), base, rank, matrix)


def unpack_kernel(at_ref, base_ref, rank_ref, *refs):
    parts, (out_ref, rows, sem) = refs[:4], refs[4:]
    zh, x, skip = at_ref[0], at_ref[1], at_ref[2]
    copies = []
    for d in range(4):
        for e in range(4):
            target = rows.at[lax.rem(zh - e + 4, 4) * 4 + lax.rem(x - d + 4, 4)]
            copies.append(pltpu.make_async_copy(parts[d].at[e], target, sem.at[d * 4 + e]))
    for copy in copies:
        copy.start()
    rank = rank_ref[...] - skip
    code = jnp.where((rank >= 0) & (rank < CAP), base_ref[...] // ROWS * CAP + rank, -1)
    columns = jnp.transpose(jnp.concatenate([code, code[: 8 - STEPS]], axis=0))
    place = lax.broadcasted_iota(jnp.int32, (NB, 16 * CAP), 1)
    for copy in copies:
        copy.wait()
    for s in range(STEPS):
        put = jnp.where(columns[:, s : s + 1] == place, 1.0, 0.0).astype(jnp.bfloat16)
        out_ref[s] = dot(put, rows[...].reshape(16 * CAP, rows.shape[2])).astype(jnp.bfloat16)


def unpack(zh, x, skip, base, rank, parts):
    width = parts[0].shape[2]
    vmem, anywhere = pl.BlockSpec(memory_space=pltpu.VMEM), pl.BlockSpec(memory_space=pl.ANY)
    return pl.pallas_call(
        unpack_kernel,
        out_shape=jax.ShapeDtypeStruct((STEPS, NB, width), jnp.bfloat16),
        in_specs=[pl.BlockSpec(memory_space=pltpu.SMEM)] + [vmem] * 2 + [anywhere] * 4,
        out_specs=vmem,
        scratch_shapes=[pltpu.VMEM((16, CAP, width), jnp.bfloat16), pltpu.SemaphoreType.DMA((16,))],
        compiler_params=pltpu.CompilerParams(vmem_limit_bytes=32 * 2**20),
        cost_estimate=pl.CostEstimate(
            flops=2 * STEPS * NB * 16 * CAP * width, bytes_accessed=4 * 2**20, transcendentals=0
        ),
    )(jnp.stack([zh, x, skip]).astype(jnp.int32), base, rank, *parts)


def body(matrix, panels, diag_blocks, pivots):
    width = matrix.shape[1]
    zh, x, y = lax.axis_index("zh"), lax.axis_index("x"), lax.axis_index("y")
    zl, c = lax.axis_index("zl"), lax.axis_index("c")
    at = jnp.stack([zh, x, zl, c]).astype(jnp.int32)
    me = zh * 4 + x
    local = me * ROWS + jnp.arange(ROWS, dtype=jnp.int32)
    t_ids = jnp.arange(STEPS, dtype=jnp.int32)
    i_ids = jnp.arange(NB, dtype=jnp.int32)

    wide, pivots, matrix = lax.optimization_barrier((jnp.broadcast_to(panels, (8,) + panels.shape), pivots, matrix))
    by_y = exchange(wide, "y")

    origin, base, rank = origins(pivots)
    packed = passed(pack(me, jnp.int32(0), base, rank, matrix), "zh")
    packed[1], packed[2], packed[3], by_y = lax.optimization_barrier((*packed[1:], by_y))

    pair = jnp.array(PAIRS, jnp.int32).reshape(8, 2, 2)
    pair = lax.dynamic_index_in_dim(pair, y // 4, 1, keepdims=False)
    swapped_at = jnp.where(origin >= 0, origin // ROWS, -1)
    ids = jnp.where(swapped_at[None] > t_ids[:, None, None], origin[None], pivots[None])
    ids = lax.dynamic_slice_in_dim(ids.reshape(STEPS * STEPS, NB), y % 4 * 64, 64, 1)
    rows = l_rows(at, pair[:, 0], pair[:, 1], ids, by_y)

    packed = passed(jnp.stack(packed), "x")
    chunk = add_up(exchange(rows, ("zl", "c")))
    chunk, pivots, diag_blocks = lax.optimization_barrier((chunk, pivots, diag_blocks))
    high, low = inverses(diag_blocks)
    chunk = add_up(everyone(chunk, "zh"))
    packed[1], packed[2], packed[3], chunk, high, low = lax.optimization_barrier((*packed[1:], chunk, high, low))
    chunk = add_up(everyone(chunk, "x"))
    panels_across = shift(by_y, "zl", 1)
    packed[0], chunk, panels_across, pivots = lax.optimization_barrier((packed[0], chunk, panels_across, pivots))
    chunk = everyone(chunk, ("y", "zl")).reshape(8, 2, 4, 16, 2 * NB)
    whole = [by_y, shift(by_y, "c", 1), panels_across, shift(panels_across, "c", 1)]
    tops = unpack(zh, x, jnp.int32(0), base, rank, packed)

    same = pivots[:, :, None, None] == pivots[None, None]
    after = (t_ids[None, :] > t_ids[:, None])[:, None, :, None]
    stays = ~jnp.any(same & after, axis=(2, 3))
    owner = jnp.where(stays, pivots // ROWS, -1)
    ahead = (owner[:, :, None] == owner[:, None, :]) & (i_ids[None, :] < i_ids[:, None])
    order = jnp.where(stays, jnp.sum(ahead, axis=2, dtype=jnp.int32), -1)
    rounds = (jnp.max(order) + SLOTS) // SLOTS
    mine = jnp.minimum(me, STEPS - 1)
    my_rank = jnp.where(me < STEPS, lax.dynamic_index_in_dim(order, mine, 0, keepdims=False), -1)
    my_owner = lax.dynamic_index_in_dim(owner, mine, 0, keepdims=False)

    def slots(q):
        n = my_rank - q * SLOTS
        return jnp.where((n >= 0) & (n < SLOTS), my_owner * SLOTS + n, -1)

    first = slots(0)[None]
    tops, chunk, whole[1], whole[3], first = lax.optimization_barrier((tops, chunk, whole[1], whole[3], first))

    def more_tops(state):
        q, tops = state
        held = pack(me, q * CAP, base, rank, matrix)
        held = everyone(held, ("zh", "x")).reshape(4, 4, CAP, width)
        held = [jnp.stack([held[(4 - e) % 4, (4 - d) % 4] for e in range(4)]) for d in range(4)]
        zero = jnp.int32(0)
        return q + 1, tops + unpack(zero, zero, q * CAP, base, rank, held)

    top_rounds = (jnp.max(rank) + CAP) // CAP
    _, tops = lax.while_loop(lambda state: state[0] < top_rounds, more_tops, (jnp.int32(1), tops))
    blocks = [chunk, shift(chunk, "c", 1)]
    u, old, send = solve(at, first, high, low, matrix, tops, blocks, whole)

    got = exchange(send.reshape(16, SLOTS, width), ("zh", "x"))
    u, pivots = lax.optimization_barrier((u, pivots))
    here = (pivots.reshape(-1)[None, :] == local[:, None]) & stays.reshape(-1)[None, :]
    tag = jnp.max(jnp.where(here, (t_ids[:, None] * NB + order).reshape(-1)[None, :], -1), axis=1)
    last = jnp.where(tag >= 0, tag // NB, -1)
    at_rank = jnp.where(tag >= 0, tag % NB, -1)

    def landing(q):
        n = at_rank - q * SLOTS
        return picks(jnp.where((n >= 0) & (n < SLOTS), last * SLOTS + n, -1), jnp.arange(STEPS * SLOTS, dtype=jnp.int32))

    def deliver(sent):
        return exchange(sent.reshape(16, SLOTS, width), ("zh", "x"))

    total = update(at, jnp.broadcast_to(last[:, None], (ROWS, 128)), u, matrix, whole)
    total, got = lax.optimization_barrier((total, got))

    def more(state):
        q, total = state
        sent = dot(picks(jnp.arange(16 * SLOTS, dtype=jnp.int32), slots(q)), old).astype(jnp.bfloat16)
        got = deliver(sent)[:STEPS].reshape(STEPS * SLOTS, width)
        return q + 1, total + dot(landing(q), got)

    _, total = lax.while_loop(lambda state: state[0] < rounds, more, (jnp.int32(1), total))
    return place(landing(0), got, total)


def solution(mesh):
    fine = Mesh(mesh.devices.reshape(4, 4, 8, 2, 2), FINE)
    prow, pcol = ("zh", "x"), ("y", "zl", "c")
    return jax.shard_map(
        body,
        mesh=fine,
        in_specs=(P(prow, pcol), P(None, prow + pcol, None), P(), P()),
        out_specs=P(prow, pcol),
        check_vma=False,
    )
```

```python
import jax
import jax.numpy as jnp
from jax import lax
from jax.experimental import pallas as pl
from jax.experimental.pallas import tpu as pltpu
from jax.sharding import Mesh
from jax.sharding import PartitionSpec as P

STEPS = 6
NB = 256
ROWS = 1024
FINE = ("zh", "x", "y", "zl", "c")
PAIRS = [(s, k) for k in range(STEPS) for s in range(k + 1, STEPS)] + [(0, 0)]
PLACE = {pair: n for n, pair in enumerate(PAIRS)}
CAP = 144
SLOTS = 32


def split(v):
    high = v.astype(jnp.bfloat16)
    return high, (v - high.astype(jnp.float32)).astype(jnp.bfloat16)


def dot(a, b):
    return jnp.dot(a, b, preferred_element_type=jnp.float32)


def dot3(a, b):
    ah, al = split(a)
    bh, bl = split(b)
    return dot(ah, bh) + (dot(ah, bl) + dot(al, bh))


def inverse_kernel(l_ref, high_ref, low_ref):
    row = lax.broadcasted_iota(jnp.int32, (NB, NB), 0)
    col = lax.broadcasted_iota(jnp.int32, (NB, NB), 1)
    eye = (row == col).astype(jnp.float32)
    lower = [l_ref[s] for s in range(STEPS)]
    inv = [eye] * STEPS
    size = 1
    while size < NB:
        joins = (row // (2 * size) == col // (2 * size)) & (row // size > col // size)
        parts = [jnp.where(joins, m, 0.0) for m in lower]
        if size == 1:
            inv = [eye - m for m in parts]
        else:
            left = [dot3(m, x) for m, x in zip(parts, inv)]
            inv = [x - dot3(x, m) for x, m in zip(inv, left)]
        size *= 2
    for s in range(STEPS):
        high_ref[s], low_ref[s] = split(inv[s])


def inverses(diag_blocks):
    out = jax.ShapeDtypeStruct((STEPS, NB, NB), jnp.bfloat16)
    spec = pl.BlockSpec(memory_space=pltpu.VMEM)
    return pl.pallas_call(
        inverse_kernel,
        out_shape=(out, out),
        in_specs=[spec],
        out_specs=(spec, spec),
        compiler_params=pltpu.CompilerParams(vmem_limit_bytes=48 * 2**20),
        cost_estimate=pl.CostEstimate(flops=2 * 42 * 6 * NB**3, bytes_accessed=3 * 2**20, transcendentals=0),
    )(diag_blocks)


def exchange(v, axis):
    return lax.all_to_all(v, axis, 0, 0)


def everyone(v, axis):
    n = lax.axis_size(axis)
    return exchange(jnp.broadcast_to(v[None], (n,) + v.shape), axis)


def add_up(v):
    return jnp.sum(v.astype(jnp.float32), axis=0).astype(v.dtype)


def shift(v, axis, by):
    n = lax.axis_size(axis)
    return lax.ppermute(v, axis, [(i, (i + by) % n) for i in range(n)])


def dealt(v, axis):
    n, at = lax.axis_size(axis), lax.axis_index(axis)
    parts = [lax.dynamic_index_in_dim(v, (at + d) % n, 0, keepdims=False) for d in range(n)]
    return parts[:1] + [shift(parts[d], axis, d) for d in range(1, n)]


def passed(v, axis):
    return [v] + [shift(v, axis, d) for d in range(1, lax.axis_size(axis))]


def picks(ids, held):
    return (ids[:, None] == held[None, :]).astype(jnp.bfloat16)


def l_rows_kernel(at_ref, ts_ref, ks_ref, ids_ref, panels_ref, out_ref):
    zh, x, zl, c = at_ref[0], at_ref[1], at_ref[2], at_ref[3]
    lane = lax.broadcasted_iota(jnp.int32, (NB, 64), 0)
    held = (zh * 4 + x) * ROWS + zl * 64 + c * 32 + lane // 32 * 128 + lane % 32
    for m in range(8):
        t, k = ts_ref[m], ks_ref[m]
        put = jnp.where(held == ids_ref[pl.ds(k * STEPS + t, 1), :], 1.0, 0.0).astype(jnp.bfloat16)
        mine = panels_ref[:, pl.ds(k, 1)].reshape(NB, NB)
        rows = lax.dot_general(put, mine, (((0,), (0,)), ((), ())), preferred_element_type=jnp.float32)
        out_ref[:, m // 2, :, m % 2 * NB : m % 2 * NB + NB] = rows.astype(jnp.bfloat16).reshape(4, 16, NB)


def l_rows(at, ts, ks, ids, panels):
    vmem, smem = pl.BlockSpec(memory_space=pltpu.VMEM), pl.BlockSpec(memory_space=pltpu.SMEM)
    return pl.pallas_call(
        l_rows_kernel,
        out_shape=jax.ShapeDtypeStruct((4, 4, 16, 2 * NB), jnp.bfloat16),
        in_specs=[smem, smem, smem, vmem, vmem],
        out_specs=vmem,
        compiler_params=pltpu.CompilerParams(vmem_limit_bytes=16 * 2**20),
        cost_estimate=pl.CostEstimate(flops=2 * 8 * 64 * NB * NB, bytes_accessed=2**20, transcendentals=0),
    )(at, ts, ks, ids, panels)


def turned(zl, c, n):
    return lax.rem(zl + n // 2, 2), lax.rem(c + n % 2, 2)


def solve_kernel(at_ref, slot_ref, high_ref, low_ref, matrix_ref, *refs):
    active_in, blocks_in, panels_in = refs[0], refs[1:3], refs[3:7]
    u_ref, old_ref, send_ref, active, blocks, panels, active_sem, blocks_sem, panels_sem = refs[7:]
    zh, x, zl, c = at_ref[0], at_ref[1], at_ref[2], at_ref[3]
    me = zh * 4 + x
    width = matrix_ref.shape[1]
    copies = [pltpu.make_async_copy(active_in, active, active_sem.at[0])]
    for n in range(2):
        target = blocks.at[:, :, lax.rem(c + n, 2)]
        copies.append(pltpu.make_async_copy(blocks_in[n], target, blocks_sem.at[n]))
    for n in range(4):
        a, b = turned(zl, c, n)
        copies.append(pltpu.make_async_copy(panels_in[n].at[0:2], panels.at[:, a, b], panels_sem.at[n]))
    for copy in copies:
        copy.start()
    for copy in copies[:1]:
        copy.wait()

    def rows_of(n):
        return active[n]

    old_ref[...] = matrix_ref[0:NB, :]
    for s in range(STEPS):
        top = rows_of(s)
        u = (dot(high_ref[s], top) + dot(low_ref[s], top)).astype(jnp.bfloat16)
        u_ref[s] = u

        if s == 0:
            for copy in copies[1:]:
                copy.wait()
        for t in range(s + 1, STEPS):
            n = PLACE[(t, s)]
            left = n // 2 % 2 * NB
            block = blocks[n % 2 * 4 : n % 2 * 4 + 4, :, :, n // 4, :, left : left + NB].reshape(NB, NB)
            less = rows_of(t).astype(jnp.float32) - dot(block, u)
            active[t] = less.astype(jnp.bfloat16)

    for s in range(STEPS - 1):

        @pl.when((s < me) & (me < STEPS))
        def _():
            panel = panels[:, :, :, s].reshape(NB, NB)
            old_ref[...] = (old_ref[...].astype(jnp.float32) - dot(panel, u_ref[s])).astype(jnp.bfloat16)

    slot = lax.broadcasted_iota(jnp.int32, (16 * SLOTS, NB), 0)
    put = jnp.where(slot == slot_ref[...], 1.0, 0.0).astype(jnp.bfloat16)
    send_ref[...] = dot(put, old_ref[...]).astype(jnp.bfloat16)


def solve(at, slot, high, low, matrix, active, blocks, panels):
    width = matrix.shape[1]
    vmem, anywhere = pl.BlockSpec(memory_space=pltpu.VMEM), pl.BlockSpec(memory_space=pl.ANY)
    return pl.pallas_call(
        solve_kernel,
        out_shape=(
            jax.ShapeDtypeStruct((STEPS, NB, width), jnp.bfloat16),
            jax.ShapeDtypeStruct((NB, width), jnp.bfloat16),
            jax.ShapeDtypeStruct((16 * SLOTS, width), jnp.bfloat16),
        ),
        in_specs=[pl.BlockSpec(memory_space=pltpu.SMEM)] + [vmem] * 4 + [anywhere] * 7,
        out_specs=(vmem,) * 3,
        scratch_shapes=[
            pltpu.VMEM((STEPS, NB, width), jnp.bfloat16),
            pltpu.VMEM((8, 2, 2, 4, 16, 2 * NB), jnp.bfloat16),
            pltpu.VMEM((2, 2, 2, STEPS, 32, NB), jnp.bfloat16),
            pltpu.SemaphoreType.DMA((1,)),
            pltpu.SemaphoreType.DMA((2,)),
            pltpu.SemaphoreType.DMA((4,)),
        ],
        compiler_params=pltpu.CompilerParams(vmem_limit_bytes=58 * 2**20),
        cost_estimate=pl.CostEstimate(flops=2 * 35 * NB * NB * width, bytes_accessed=9 * 2**20, transcendentals=0),
    )(at, slot, high, low, matrix, active, *blocks, *panels)


def update_kernel(at_ref, last_ref, u_ref, matrix_ref, *refs):
    panels_in, (out_ref, panels, panels_sem) = refs[:4], refs[4:]
    zl, c = at_ref[2], at_ref[3]
    width = matrix_ref.shape[1]
    copies = []
    for n in range(4):
        a, b = turned(zl, c, n)
        copies.append(pltpu.make_async_copy(panels_in[n], panels.at[:, a, b], panels_sem.at[n]))
    for copy in copies:
        copy.start()
    for copy in copies:
        copy.wait()
    tall = 256

    @pl.loop(0, ROWS // tall)
    def _(i):
        span = pl.ds(pl.multiple_of(i * tall, tall), tall)
        last = jnp.concatenate([last_ref[span, :]] * (width // 128), axis=1)
        rows = matrix_ref[span, :].astype(jnp.float32)
        for s in range(STEPS):
            panel = panels[pl.ds(i * (tall // 128), tall // 128), :, :, s].reshape(tall, NB)
            rows = jnp.where(last == s, 0.0, rows) - dot(panel, u_ref[s])
            rows = jnp.where(last >= 0, rows, rows.astype(jnp.bfloat16).astype(jnp.float32))
        out_ref[span, :] = rows

    me = at_ref[0] * 4 + at_ref[1]

    @pl.when(me < STEPS)
    def _():
        own = u_ref[pl.ds(jnp.minimum(me, STEPS - 1), 1)].reshape(NB, width)
        out_ref[0:NB, :] = own.astype(jnp.float32)


def update(at, last, u, matrix, panels):
    vmem, anywhere = pl.BlockSpec(memory_space=pltpu.VMEM), pl.BlockSpec(memory_space=pl.ANY)
    return pl.pallas_call(
        update_kernel,
        out_shape=jax.ShapeDtypeStruct(matrix.shape, jnp.float32),
        in_specs=[pl.BlockSpec(memory_space=pltpu.SMEM)] + [vmem] * 3 + [anywhere] * 4,
        out_specs=vmem,
        scratch_shapes=[pltpu.VMEM((8, 2, 2, STEPS, 32, NB), jnp.bfloat16), pltpu.SemaphoreType.DMA((4,))],
        compiler_params=pltpu.CompilerParams(vmem_limit_bytes=58 * 2**20),
        cost_estimate=pl.CostEstimate(
            flops=2 * matrix.size * STEPS * NB, bytes_accessed=8 * 2**20, transcendentals=0
        ),
    )(at, last, u, matrix, *panels)


def place_kernel(put_ref, got_ref, total_ref, out_ref):
    width = out_ref.shape[1]
    got = got_ref[0:STEPS].reshape(STEPS * SLOTS, width)
    out_ref[...] = (total_ref[...] + dot(put_ref[...], got)).astype(jnp.bfloat16)


def place(put, got, total):
    vmem = pl.BlockSpec(memory_space=pltpu.VMEM)
    return pl.pallas_call(
        place_kernel,
        out_shape=jax.ShapeDtypeStruct(total.shape, jnp.bfloat16),
        in_specs=[vmem] * 3,
        out_specs=vmem,
        compiler_params=pltpu.CompilerParams(vmem_limit_bytes=32 * 2**20),
        cost_estimate=pl.CostEstimate(
            flops=2 * total.size * STEPS * SLOTS, bytes_accessed=6 * 2**20, transcendentals=0
        ),
    )(put, got, total)


def origin_kernel(pivots_ref, origin_ref, base_ref, rank_ref):
    rows = pivots_ref[...]
    columns = jnp.transpose(jnp.concatenate([rows, rows[: 8 - STEPS]], axis=0))
    down = lax.broadcasted_iota(jnp.int32, (NB, NB), 0)
    index = down.astype(jnp.float32)
    earlier = jnp.where(down < lax.broadcasted_iota(jnp.int32, (NB, NB), 1), 1.0, 0.0).astype(jnp.bfloat16)
    prow = lax.broadcasted_iota(jnp.int32, (16, NB), 0)
    so_far = jnp.zeros((16, 1), jnp.float32)
    for s in range(STEPS):
        row = rows[s : s + 1]
        latest = jnp.full((1, NB), -1.0, jnp.float32)
        for t in range(s):
            code = jnp.where(columns[:, t : t + 1] == row, index + float(t * ROWS), -1.0)
            latest = jnp.maximum(latest, jnp.max(code, axis=0, keepdims=True))
        latest = latest.astype(jnp.int32)
        base = jnp.where(latest >= 0, latest, row)
        origin_ref[s : s + 1, :] = latest
        base_ref[s : s + 1, :] = base
        holds = jnp.where(prow == base // ROWS, 1.0, 0.0)
        ahead = dot(holds.astype(jnp.bfloat16), earlier) + so_far
        rank_ref[s : s + 1, :] = jnp.sum(holds * ahead, axis=0, keepdims=True).astype(jnp.int32)
        so_far = so_far + jnp.sum(holds, axis=1, keepdims=True)


def origins(pivots):
    vmem = pl.BlockSpec(memory_space=pltpu.VMEM)
    out = jax.ShapeDtypeStruct(pivots.shape, jnp.int32)
    return pl.pallas_call(
        origin_kernel,
        out_shape=(out,) * 3,
        in_specs=[vmem],
        out_specs=(vmem,) * 3,
        compiler_params=pltpu.CompilerParams(vmem_limit_bytes=16 * 2**20),
        cost_estimate=pl.CostEstimate(flops=1000, bytes_accessed=20000, transcendentals=0),
    )(pivots)


def pack_kernel(at_ref, base_ref, rank_ref, matrix_ref, out_ref):
    me, skip = at_ref[0], at_ref[1]
    slot = lax.broadcasted_iota(jnp.int32, (CAP, NB), 0)
    ids = jnp.zeros((CAP, 1), jnp.float32)
    for s in range(STEPS):
        base = base_ref[s : s + 1, :]
        code = jnp.where(base // ROWS == me, rank_ref[s : s + 1, :] - skip, -1)
        ids = ids + jnp.sum(jnp.where(slot == code, (base + 1).astype(jnp.float32), 0.0), axis=1, keepdims=True)
    local = ids.astype(jnp.int32) - 1 - me * ROWS
    put = jnp.where(lax.broadcasted_iota(jnp.int32, (CAP, ROWS), 1) == local, 1.0, 0.0).astype(jnp.bfloat16)
    out_ref[...] = dot(put, matrix_ref[...]).astype(jnp.bfloat16)


def pack(me, skip, base, rank, matrix):
    vmem = pl.BlockSpec(memory_space=pltpu.VMEM)
    return pl.pallas_call(
        pack_kernel,
        out_shape=jax.ShapeDtypeStruct((CAP, matrix.shape[1]), jnp.bfloat16),
        in_specs=[pl.BlockSpec(memory_space=pltpu.SMEM)] + [vmem] * 3,
        out_specs=vmem,
        compiler_params=pltpu.CompilerParams(vmem_limit_bytes=16 * 2**20),
        cost_estimate=pl.CostEstimate(flops=2 * CAP * matrix.size, bytes_accessed=2**20, transcendentals=0),
    )(jnp.stack([me, skip]).astype(jnp.int32), base, rank, matrix)


def unpack_kernel(at_ref, base_ref, rank_ref, *refs):
    parts, (out_ref, rows, sem) = refs[:4], refs[4:]
    zh, x, skip = at_ref[0], at_ref[1], at_ref[2]
    copies = []
    for d in range(4):
        for e in range(4):
            target = rows.at[lax.rem(zh - e + 4, 4) * 4 + lax.rem(x - d + 4, 4)]
            copies.append(pltpu.make_async_copy(parts[d].at[e], target, sem.at[d * 4 + e]))
    for copy in copies:
        copy.start()
    rank = rank_ref[...] - skip
    code = jnp.where((rank >= 0) & (rank < CAP), base_ref[...] // ROWS * CAP + rank, -1)
    columns = jnp.transpose(jnp.concatenate([code, code[: 8 - STEPS]], axis=0))
    place = lax.broadcasted_iota(jnp.int32, (NB, 16 * CAP), 1)
    for copy in copies:
        copy.wait()
    for s in range(STEPS):
        put = jnp.where(columns[:, s : s + 1] == place, 1.0, 0.0).astype(jnp.bfloat16)
        out_ref[s] = dot(put, rows[...].reshape(16 * CAP, rows.shape[2])).astype(jnp.bfloat16)


def unpack(zh, x, skip, base, rank, parts):
    width = parts[0].shape[2]
    vmem, anywhere = pl.BlockSpec(memory_space=pltpu.VMEM), pl.BlockSpec(memory_space=pl.ANY)
    return pl.pallas_call(
        unpack_kernel,
        out_shape=jax.ShapeDtypeStruct((STEPS, NB, width), jnp.bfloat16),
        in_specs=[pl.BlockSpec(memory_space=pltpu.SMEM)] + [vmem] * 2 + [anywhere] * 4,
        out_specs=vmem,
        scratch_shapes=[pltpu.VMEM((16, CAP, width), jnp.bfloat16), pltpu.SemaphoreType.DMA((16,))],
        compiler_params=pltpu.CompilerParams(vmem_limit_bytes=32 * 2**20),
        cost_estimate=pl.CostEstimate(
            flops=2 * STEPS * NB * 16 * CAP * width, bytes_accessed=4 * 2**20, transcendentals=0
        ),
    )(jnp.stack([zh, x, skip]).astype(jnp.int32), base, rank, *parts)


def body(matrix, panels, diag_blocks, pivots):
    width = matrix.shape[1]
    zh, x, y = lax.axis_index("zh"), lax.axis_index("x"), lax.axis_index("y")
    zl, c = lax.axis_index("zl"), lax.axis_index("c")
    at = jnp.stack([zh, x, zl, c]).astype(jnp.int32)
    me = zh * 4 + x
    local = me * ROWS + jnp.arange(ROWS, dtype=jnp.int32)
    t_ids = jnp.arange(STEPS, dtype=jnp.int32)
    i_ids = jnp.arange(NB, dtype=jnp.int32)

    wide, pivots, matrix = lax.optimization_barrier((jnp.broadcast_to(panels, (8,) + panels.shape), pivots, matrix))
    by_y = exchange(wide, "y")

    origin, base, rank = origins(pivots)
    packed = passed(pack(me, jnp.int32(0), base, rank, matrix), "zh")
    packed[1], packed[2], packed[3], by_y = lax.optimization_barrier((*packed[1:], by_y))

    pair = jnp.array(PAIRS, jnp.int32).reshape(8, 2, 2)
    pair = lax.dynamic_index_in_dim(pair, y // 4, 1, keepdims=False)
    swapped_at = jnp.where(origin >= 0, origin // ROWS, -1)
    ids = jnp.where(swapped_at[None] > t_ids[:, None, None], origin[None], pivots[None])
    ids = lax.dynamic_slice_in_dim(ids.reshape(STEPS * STEPS, NB), y % 4 * 64, 64, 1)
    rows = l_rows(at, pair[:, 0], pair[:, 1], ids, by_y)

    packed = jnp.stack(packed)
    chunk = add_up(exchange(rows, ("zl", "c")))
    packed, chunk, pivots, diag_blocks = lax.optimization_barrier((packed, chunk, pivots, diag_blocks))
    packed = passed(packed, "x")
    high, low = inverses(diag_blocks)
    chunk = add_up(everyone(chunk, "zh"))
    chunk, high, low = lax.optimization_barrier((chunk, high, low))
    chunk = add_up(everyone(chunk, "x"))
    panels_across = shift(by_y, "zl", 1)
    *packed, chunk, panels_across, pivots = lax.optimization_barrier((*packed, chunk, panels_across, pivots))
    chunk = everyone(chunk, ("y", "zl")).reshape(8, 2, 4, 16, 2 * NB)
    whole = [by_y, shift(by_y, "c", 1), panels_across, shift(panels_across, "c", 1)]
    tops = unpack(zh, x, jnp.int32(0), base, rank, packed)

    same = pivots[:, :, None, None] == pivots[None, None]
    after = (t_ids[None, :] > t_ids[:, None])[:, None, :, None]
    stays = ~jnp.any(same & after, axis=(2, 3))
    owner = jnp.where(stays, pivots // ROWS, -1)
    ahead = (owner[:, :, None] == owner[:, None, :]) & (i_ids[None, :] < i_ids[:, None])
    order = jnp.where(stays, jnp.sum(ahead, axis=2, dtype=jnp.int32), -1)
    rounds = (jnp.max(order) + SLOTS) // SLOTS
    mine = jnp.minimum(me, STEPS - 1)
    my_rank = jnp.where(me < STEPS, lax.dynamic_index_in_dim(order, mine, 0, keepdims=False), -1)
    my_owner = lax.dynamic_index_in_dim(owner, mine, 0, keepdims=False)

    def slots(q):
        n = my_rank - q * SLOTS
        return jnp.where((n >= 0) & (n < SLOTS), my_owner * SLOTS + n, -1)

    first = slots(0)[None]
    tops, chunk, whole[1], whole[3], first = lax.optimization_barrier((tops, chunk, whole[1], whole[3], first))

    def more_tops(state):
        q, tops = state
        held = pack(me, q * CAP, base, rank, matrix)
        held = everyone(held, ("zh", "x")).reshape(4, 4, CAP, width)
        held = [jnp.stack([held[(4 - e) % 4, (4 - d) % 4] for e in range(4)]) for d in range(4)]
        zero = jnp.int32(0)
        return q + 1, tops + unpack(zero, zero, q * CAP, base, rank, held)

    top_rounds = (jnp.max(rank) + CAP) // CAP
    _, tops = lax.while_loop(lambda state: state[0] < top_rounds, more_tops, (jnp.int32(1), tops))
    blocks = [chunk, shift(chunk, "c", 1)]
    u, old, send = solve(at, first, high, low, matrix, tops, blocks, whole)

    got = exchange(send.reshape(16, SLOTS, width), ("zh", "x"))
    u, pivots = lax.optimization_barrier((u, pivots))
    here = (pivots.reshape(-1)[None, :] == local[:, None]) & stays.reshape(-1)[None, :]
    tag = jnp.max(jnp.where(here, (t_ids[:, None] * NB + order).reshape(-1)[None, :], -1), axis=1)
    last = jnp.where(tag >= 0, tag // NB, -1)
    at_rank = jnp.where(tag >= 0, tag % NB, -1)

    def landing(q):
        n = at_rank - q * SLOTS
        return picks(jnp.where((n >= 0) & (n < SLOTS), last * SLOTS + n, -1), jnp.arange(STEPS * SLOTS, dtype=jnp.int32))

    def deliver(sent):
        return exchange(sent.reshape(16, SLOTS, width), ("zh", "x"))

    total = update(at, jnp.broadcast_to(last[:, None], (ROWS, 128)), u, matrix, whole)
    total, got = lax.optimization_barrier((total, got))

    def more(state):
        q, total = state
        sent = dot(picks(jnp.arange(16 * SLOTS, dtype=jnp.int32), slots(q)), old).astype(jnp.bfloat16)
        got = deliver(sent)[:STEPS].reshape(STEPS * SLOTS, width)
        return q + 1, total + dot(landing(q), got)

    _, total = lax.while_loop(lambda state: state[0] < rounds, more, (jnp.int32(1), total))
    return place(landing(0), got, total)


def solution(mesh):
    fine = Mesh(mesh.devices.reshape(4, 4, 8, 2, 2), FINE)
    prow, pcol = ("zh", "x"), ("y", "zl", "c")
    return jax.shard_map(
        body,
        mesh=fine,
        in_specs=(P(prow, pcol), P(None, prow + pcol, None), P(), P()),
        out_specs=P(prow, pcol),
        check_vma=False,
    )
```
